32 devices in a mesh: dp: 8 (over z, x), chan: 4 (over y, core).
Axes of the slice: x: 2, y: 2, z: 4, core: 2. Of those that a mesh axis runs over, the one named last changes fastest.
Arguments:
- images: bfloat16 [64, 14, 14, 1024], P('dp', None, None, 'chan'), may hold values from -6 to 6
- out_grad: bfloat16 [64, 7, 7, 2048], P('dp', None, None, 'chan'), may hold values from -6 to 6
- crop_width: int32 [64], P('dp'), may hold values from 0 to 3, as said below
- width_bound: int32 [4], replicated, may hold values from 128 to 512, as said below
- depth_gate: int32 [4], replicated, may hold values from 0 to 1, as said below
- first_reduce: bfloat16 [1024, 512], P(None, 'chan'), may hold values from -0.1875 to 0.1875
- first_reduce_gain: float32 [4, 512], P(None, 'chan'), may hold values from 0.5 to 1.5
- first_reduce_shift: float32 [4, 512], P(None, 'chan'), may hold values from -3 to 3
- first_spatial: bfloat16 [3, 3, 512, 512], P(None, None, None, 'chan'), may hold values from -0.09375 to 0.09375
- first_spatial_gain: float32 [4, 512], P(None, 'chan'), may hold values from 0.5 to 1.5
- first_spatial_shift: float32 [4, 512], P(None, 'chan'), may hold values from -3 to 3
- first_expand: bfloat16 [512, 2048], P('chan'), may hold values from -0.25 to 0.25
- first_expand_gain: float32 [4, 2048], P(None, 'chan'), may hold values from 0.5 to 1.5
- first_expand_shift: float32 [4, 2048], P(None, 'chan'), may hold values from -3 to 3
- first_project: bfloat16 [1024, 2048], P(None, 'chan'), may hold values from -0.1875 to 0.1875
- first_project_gain: float32 [4, 2048], P(None, 'chan'), may hold values from 0.5 to 1.5
- first_project_shift: float32 [4, 2048], P(None, 'chan'), may hold values from -3 to 3
- second_reduce: bfloat16 [2048, 512], P(None, 'chan'), may hold values from -0.125 to 0.125
- second_reduce_gain: float32 [4, 512], P(None, 'chan'), may hold values from 0.5 to 1.5
- second_reduce_shift: float32 [4, 512], P(None, 'chan'), may hold values from -3 to 3
- second_spatial: bfloat16 [3, 3, 512, 512], P(None, None, None, 'chan'), may hold values from -0.09375 to 0.09375
- second_spatial_gain: float32 [4, 512], P(None, 'chan'), may hold values from 0.5 to 1.5
- second_spatial_shift: float32 [4, 512], P(None, 'chan'), may hold values from -3 to 3
- second_expand: bfloat16 [512, 2048], P('chan'), may hold values from -0.25 to 0.25
- second_expand_gain: float32 [4, 2048], P(None, 'chan'), may hold values from 0.5 to 1.5
- second_expand_shift: float32 [4, 2048], P(None, 'chan'), may hold values from -3 to 3
Outputs:
- result: bfloat16 [64, 7, 7, 2048], P('dp', None, None, 'chan')
- images_grad: float32 [64, 14, 14, 1024], P('dp', None, None, 'chan')
- first_reduce_grad: float32 [1024, 512], P(None, 'chan')
- first_reduce_gain_grad: float32 [4, 512], P(None, 'chan')
- first_reduce_shift_grad: float32 [4, 512], P(None, 'chan')
- first_spatial_grad: float32 [3, 3, 512, 512], P(None, None, None, 'chan')
- first_spatial_gain_grad: float32 [4, 512], P(None, 'chan')
- first_spatial_shift_grad: float32 [4, 512], P(None, 'chan')
- first_expand_grad: float32 [512, 2048], P('chan')
- first_expand_gain_grad: float32 [4, 2048], P(None, 'chan')
- first_expand_shift_grad: float32 [4, 2048], P(None, 'chan')
- first_project_grad: float32 [1024, 2048], P(None, 'chan')
- first_project_gain_grad: float32 [4, 2048], P(None, 'chan')
- first_project_shift_grad: float32 [4, 2048], P(None, 'chan')
- second_reduce_grad: float32 [2048, 512], P(None, 'chan')
- second_reduce_gain_grad: float32 [4, 512], P(None, 'chan')
- second_reduce_shift_grad: float32 [4, 512], P(None, 'chan')
- second_spatial_grad: float32 [3, 3, 512, 512], P(None, None, None, 'chan')
- second_spatial_gain_grad: float32 [4, 512], P(None, 'chan')
- second_spatial_shift_grad: float32 [4, 512], P(None, 'chan')
- second_expand_grad: float32 [512, 2048], P('chan')
- second_expand_gain_grad: float32 [4, 2048], P(None, 'chan')
- second_expand_shift_grad: float32 [4, 2048], P(None, 'chan')
The draws below stay inside these ranges and needn't reach their ends.
Inputs may be any that keep to these rules, and one draw needn't show every extreme that they name: `crop_width`: each of the 4 widths is taken by at least one crop. `width_bound`: a multiple of 32; one width uses all 512 channels and another 512 // 4. `depth_gate`: the width with all 512 channels runs the second block, the width with 128 channels skips it.
All inputs are finite; a program needn't handle non-finite values.
Results may differ from the reference program's by a relative error of at most 0.029.
Values may be sent and summed in bfloat16 or wider, within the bound.
No kernel may reach another device: no remote copies, remote signals or barrier semaphores. Data moves between devices by JAX's collectives and lax.ppermute only.
A program may use at most 128 MiB of HBM per device.

```python
import jax
import jax.numpy as jnp
from jax import lax

IN = 1024
MID = 512
OUT = 2048
WIDTHS = 4
SIDE = 14
CROPS = 64


def width_order(key):
    return jax.random.permutation(jax.random.fold_in(key, 7), WIDTHS)


def draw_crop_width(key, part):
    key = jax.random.fold_in(key, 1)
    first_key, second_key = jax.random.split(key)
    chosen = jax.random.randint(first_key, (CROPS,), 0, WIDTHS)
    return chosen.at[:WIDTHS].set(jax.random.permutation(second_key, WIDTHS)).astype(jnp.int32)


def draw_width_bound(key, part):
    order = width_order(key)
    key = jax.random.fold_in(key, 2)
    levels = jax.random.randint(key, (WIDTHS,), 4, 17)
    levels = levels.at[order[0]].set(16).at[order[1]].set(4)
    return (levels * (MID // 16)).astype(jnp.int32)


def draw_depth_gate(key, part):
    order = width_order(key)
    key = jax.random.fold_in(key, 3)
    gates = jax.random.randint(key, (WIDTHS,), 0, 2)
    return gates.at[order[0]].set(1).at[order[1]].set(0).astype(jnp.int32)


def level_of(stream_key, extent, cuts, least, top_value):
    factor_of = 1.0
    for position, shards_of in cuts:
        draws = jax.random.uniform(jax.random.fold_in(jax.random.fold_in(stream_key, 6), position), (shards_of,), jnp.float32, least / len(cuts), top_value / len(cuts))
        factor_of = factor_of * jnp.repeat(jnp.exp(draws), extent[position] // shards_of).reshape((-1,) + (1,) * (len(extent) - 1 - position))
    return factor_of


def scatter_about(rng, extent, scale, bound, pieces=(), held_as=jnp.bfloat16):
    entries = jax.random.normal(rng, extent, jnp.float32) * scale
    if len(pieces) > 0:
        entries = level_of(rng, extent, pieces, -0.22, 0.18) * entries
    return jnp.clip(entries, min=-bound, max=bound).astype(held_as)


def setup_inputs(seed: int = 0) -> dict:
    splits = jax.random.split(jax.random.key(seed), 27)
    images = scatter_about(splits[0], (CROPS, SIDE, SIDE, IN), 1.0, 6.0, ((0, 8), (3, 4)))
    out_grad = scatter_about(splits[1], (CROPS, SIDE // 2, SIDE // 2, OUT), 1.0, 6.0, ((0, 8), (3, 4)))
    crop_width = draw_crop_width(jax.random.fold_in(splits[26], 71), 0)
    width_bound = draw_width_bound(jax.random.fold_in(splits[26], 71), 0)
    depth_gate = draw_depth_gate(jax.random.fold_in(splits[26], 71), 0)
    first_reduce = scatter_about(splits[5], (IN, MID), IN ** -0.5, 0.1875, ((1, 4),))
    first_reduce_gain = jnp.clip(1.0 + 0.1 * jax.random.normal(splits[6], (WIDTHS, MID), jnp.float32), 0.5, 1.5)
    first_reduce_shift = scatter_about(splits[7], (WIDTHS, MID), 0.5, 3.0, ((1, 4),), jnp.float32)
    first_spatial = scatter_about(splits[8], (3, 3, MID, MID), (9 * MID) ** -0.5, 0.09375, ((3, 4),))
    first_spatial_gain = jnp.clip(1.0 + 0.1 * jax.random.normal(splits[9], (WIDTHS, MID), jnp.float32), 0.5, 1.5)
    first_spatial_shift = scatter_about(splits[10], (WIDTHS, MID), 0.5, 3.0, ((1, 4),), jnp.float32)
    first_expand = scatter_about(splits[11], (MID, OUT), MID ** -0.5, 0.25, ((0, 4),))
    first_expand_gain = jnp.clip(1.0 + 0.1 * jax.random.normal(splits[12], (WIDTHS, OUT), jnp.float32), 0.5, 1.5)
    first_expand_shift = scatter_about(splits[13], (WIDTHS, OUT), 0.5, 3.0, ((1, 4),), jnp.float32)
    first_project = scatter_about(splits[14], (IN, OUT), IN ** -0.5, 0.1875, ((1, 4),))
    first_project_gain = jnp.clip(1.0 + 0.1 * jax.random.normal(splits[15], (WIDTHS, OUT), jnp.float32), 0.5, 1.5)
    first_project_shift = scatter_about(splits[16], (WIDTHS, OUT), 0.5, 3.0, ((1, 4),), jnp.float32)
    second_reduce = scatter_about(splits[17], (OUT, MID), OUT ** -0.5, 0.125, ((1, 4),))
    second_reduce_gain = jnp.clip(1.0 + 0.1 * jax.random.normal(splits[18], (WIDTHS, MID), jnp.float32), 0.5, 1.5)
    second_reduce_shift = scatter_about(splits[19], (WIDTHS, MID), 0.5, 3.0, ((1, 4),), jnp.float32)
    second_spatial = scatter_about(splits[20], (3, 3, MID, MID), (9 * MID) ** -0.5, 0.09375, ((3, 4),))
    second_spatial_gain = jnp.clip(1.0 + 0.1 * jax.random.normal(splits[21], (WIDTHS, MID), jnp.float32), 0.5, 1.5)
    second_spatial_shift = scatter_about(splits[22], (WIDTHS, MID), 0.5, 3.0, ((1, 4),), jnp.float32)
    second_expand = scatter_about(splits[23], (MID, OUT), MID ** -0.5, 0.25, ((0, 4),))
    second_expand_gain = jnp.clip(1.0 + 0.1 * jax.random.normal(splits[24], (WIDTHS, OUT), jnp.float32), 0.5, 1.5)
    second_expand_shift = scatter_about(splits[25], (WIDTHS, OUT), 0.5, 3.0, ((1, 4),), jnp.float32)
    return dict(images=images, out_grad=out_grad, crop_width=crop_width, width_bound=width_bound, depth_gate=depth_gate, first_reduce=first_reduce, first_reduce_gain=first_reduce_gain, first_reduce_shift=first_reduce_shift, first_spatial=first_spatial, first_spatial_gain=first_spatial_gain, first_spatial_shift=first_spatial_shift, first_expand=first_expand, first_expand_gain=first_expand_gain, first_expand_shift=first_expand_shift, first_project=first_project, first_project_gain=first_project_gain, first_project_shift=first_project_shift, second_reduce=second_reduce, second_reduce_gain=second_reduce_gain, second_reduce_shift=second_reduce_shift, second_spatial=second_spatial, second_spatial_gain=second_spatial_gain, second_spatial_shift=second_spatial_shift, second_expand=second_expand, second_expand_gain=second_expand_gain, second_expand_shift=second_expand_shift)


@jax.custom_vjp
def low(v):
    return lax.optimization_barrier(v.astype(jnp.bfloat16)).astype(jnp.float32)

@jax.custom_vjp
def low_back(v):
    return v

def low_keep(v):
    return (low(v), None)

def low_pass(kept, grad):
    return (grad,)

def back_keep(v):
    return (v, None)

def back_low(kept, grad):
    return (low(grad),)
low.defvjp(low_keep, low_pass)
low_back.defvjp(back_keep, back_low)
HIGHEST = lax.Precision.HIGHEST
EPSILON = 1e-05

def pointwise(source, weight):
    return jnp.einsum('bhwc,cd->bhwd', source, weight, precision=HIGHEST)

def spatial(source, kernel, stride):
    return lax.conv_general_dilated(source, kernel, (stride, stride), ((1, 1), (1, 1)), dimension_numbers=('NHWC', 'HWIO', 'NHWC'), precision=HIGHEST)

def normalize(source, gain_table, shift_table, member, counts):
    totals = (counts * (source.shape[1] * source.shape[2]))[:, None]
    sum_table = jnp.dot(member.T, lax.optimization_barrier(jnp.sum(source, axis=(1, 2))), precision=HIGHEST)
    squares = jnp.dot(member.T, lax.optimization_barrier(jnp.sum(source * source, axis=(1, 2))), precision=HIGHEST)
    average = sum_table / totals
    inverse = lax.rsqrt(squares / totals - average * average + EPSILON)
    factor = gain_table * inverse
    offset = shift_table - average * factor
    factor_rows = jnp.dot(member, factor, precision=HIGHEST)
    offset_rows = jnp.dot(member, offset, precision=HIGHEST)
    return source * factor_rows[:, None, None, :] + offset_rows[:, None, None, :]

def bottleneck(source, reduce_weight, reduce_gain, reduce_shift, spatial_weight, spatial_gain, spatial_shift, expand_weight, expand_gain, expand_shift, member, counts, width_mask, stride):
    channel_mask = width_mask[:, None, None, :]
    reduced = low_back(pointwise(source, reduce_weight))
    first_hidden = low(jax.nn.silu(normalize(reduced, reduce_gain, reduce_shift, member, counts)) * channel_mask)
    spatial_out = low_back(spatial(first_hidden, spatial_weight, stride))
    second_hidden = low(jax.nn.silu(normalize(spatial_out, spatial_gain, spatial_shift, member, counts)) * channel_mask)
    expanded = low_back(pointwise(second_hidden, expand_weight))
    return normalize(expanded, expand_gain, expand_shift, member, counts)

def network(values, member, counts, width_mask, gate_rows):
    images = values[0]
    first_block = values[1:10]
    project_weight, project_gain, project_shift = values[10:13]
    second_block = values[13:22]
    branch = bottleneck(images, *first_block, member, counts, width_mask, 2)
    projected = low_back(pointwise(images[:, ::2, ::2, :], project_weight))
    shortcut = normalize(projected, project_gain, project_shift, member, counts)
    first_out = low(jax.nn.silu(shortcut + branch))
    second_branch = bottleneck(first_out, *second_block, member, counts, width_mask, 1)
    return jax.nn.silu(first_out + gate_rows[:, None, None, None] * second_branch)

def reference(images, out_grad, crop_width, width_bound, depth_gate, first_reduce, first_reduce_gain, first_reduce_shift, first_spatial, first_spatial_gain, first_spatial_shift, first_expand, first_expand_gain, first_expand_shift, first_project, first_project_gain, first_project_shift, second_reduce, second_reduce_gain, second_reduce_shift, second_spatial, second_spatial_gain, second_spatial_shift, second_expand, second_expand_gain, second_expand_shift):
    member = (crop_width[:, None] == jnp.arange(WIDTHS, dtype=jnp.int32)[None, :]).astype(jnp.float32)
    counts = lax.optimization_barrier(jnp.sum(member, axis=0))
    bound_rows = jnp.dot(member, width_bound.astype(jnp.float32), precision=HIGHEST)
    width_mask = (jnp.arange(MID).astype(jnp.float32)[None, :] < bound_rows[:, None]).astype(jnp.float32)
    gate_rows = jnp.dot(member, depth_gate.astype(jnp.float32), precision=HIGHEST)
    primals = tuple((operand.astype(jnp.float32) for operand in (images, first_reduce, first_reduce_gain, first_reduce_shift, first_spatial, first_spatial_gain, first_spatial_shift, first_expand, first_expand_gain, first_expand_shift, first_project, first_project_gain, first_project_shift, second_reduce, second_reduce_gain, second_reduce_shift, second_spatial, second_spatial_gain, second_spatial_shift, second_expand, second_expand_gain, second_expand_shift)))

    def run(*values):
        return network(values, member, counts, width_mask, gate_rows)
    output, pullback = jax.vjp(run, *primals)
    images_grad, first_reduce_grad, first_reduce_gain_grad, first_reduce_shift_grad, first_spatial_grad, first_spatial_gain_grad, first_spatial_shift_grad, first_expand_grad, first_expand_gain_grad, first_expand_shift_grad, first_project_grad, first_project_gain_grad, first_project_shift_grad, second_reduce_grad, second_reduce_gain_grad, second_reduce_shift_grad, second_spatial_grad, second_spatial_gain_grad, second_spatial_shift_grad, second_expand_grad, second_expand_gain_grad, second_expand_shift_grad = pullback(out_grad.astype(jnp.float32))
    return (output.astype(jnp.bfloat16), images_grad, first_reduce_grad, first_reduce_gain_grad, first_reduce_shift_grad, first_spatial_grad, first_spatial_gain_grad, first_spatial_shift_grad, first_expand_grad, first_expand_gain_grad, first_expand_shift_grad, first_project_grad, first_project_gain_grad, first_project_shift_grad, second_reduce_grad, second_reduce_gain_grad, second_reduce_shift_grad, second_spatial_grad, second_spatial_gain_grad, second_spatial_shift_grad, second_expand_grad, second_expand_gain_grad, second_expand_shift_grad)
```

```python
import jax
import jax.numpy as jnp
from jax import lax
from jax.sharding import PartitionSpec as P

HIGHEST = lax.Precision.HIGHEST
EPSILON = 1e-05
LAYOUT = ("NHWC", "HWIO", "NHWC")


def silu_slope(values):
    sigmoid_value = jax.nn.sigmoid(values)
    return sigmoid_value * (1.0 + values * (1.0 - sigmoid_value))


def per_width(member, source):
    return jnp.dot(member.T, jnp.sum(source, axis=(1, 2)), precision=HIGHEST)


def to_rows(member, table):
    return jnp.dot(member, table, precision=HIGHEST)[:, None, None, :]


def dp_total(values):
    size = lax.axis_size("dp")
    copies = jnp.broadcast_to(values[None], (size,) + values.shape)
    return jnp.sum(lax.all_to_all(copies, "dp", 0, 0), axis=0)


def swap(values, axis, distance):
    size = lax.axis_size(axis)
    return lax.ppermute(values, axis, [(i, i ^ distance) for i in range(size)])


def gather_blocks(values):
    across = swap(values, "chan", 2)
    beside = swap(values, "chan", 1)
    corner = swap(across, "chan", 1)
    return jnp.concatenate([values, beside, across, corner], axis=-1)


def scatter_blocks(partial_sum):
    block = partial_sum.shape[-1] // 4
    parts = [partial_sum[..., j * block : (j + 1) * block] for j in range(4)]
    outgoing = jnp.concatenate([parts[1], parts[3]], axis=-1).astype(jnp.bfloat16)
    incoming = swap(outgoing, "chan", 1).astype(jnp.float32)
    passed = (parts[2] + incoming[..., block:]).astype(jnp.bfloat16)
    return parts[0] + incoming[..., :block] + swap(passed, "chan", 2).astype(jnp.float32)


def exchange_blocks(blocks):
    return jnp.stack([blocks[0]] + [swap(blocks[j], "chan", j) for j in range(1, 4)])


def relative(blocks, own):
    return jnp.stack(
        [lax.dynamic_index_in_dim(blocks, own ^ j, 0, keepdims=False) for j in range(4)]
    )


def dp_sum_wide(values):
    size = lax.axis_size("dp")
    place = lax.axis_index("dp")
    held = values
    distances = []
    distance = 1
    while distance < size:
        distances.append(distance)
        distance *= 2
    for distance in distances:
        bit = (place // distance) % 2
        halves = held.reshape((2, held.shape[0] // 2) + held.shape[1:])
        kept = lax.dynamic_index_in_dim(halves, bit, 0, keepdims=False)
        given = lax.dynamic_index_in_dim(halves, 1 - bit, 0, keepdims=False)
        held = (
            kept.astype(jnp.float32) + swap(given, "dp", distance).astype(jnp.float32)
        ).astype(jnp.bfloat16)
    for distance in reversed(distances):
        bit = (place // distance) % 2
        other = swap(held, "dp", distance)
        held = jnp.concatenate(
            [jnp.where(bit == 0, held, other), jnp.where(bit == 0, other, held)], axis=0
        )
    return held


def norm_forward(source, gain_table, shift_table, member, counts):
    totals = (counts * (source.shape[1] * source.shape[2]))[:, None]
    sum_table, squares = dp_total(
        jnp.stack([per_width(member, source), per_width(member, source * source)])
    )
    average = sum_table / totals
    inverse = lax.rsqrt(squares / totals - average * average + EPSILON)
    factor = gain_table * inverse
    offset = shift_table - average * factor
    normed = source * to_rows(member, factor) + to_rows(member, offset)
    return (normed, (average, inverse))


def norm_backward(upstream, source, stored, gain_table, member, counts):
    average, inverse = stored
    totals = (counts * (source.shape[1] * source.shape[2]))[:, None]
    centered = (source - to_rows(member, average)) * to_rows(member, inverse)
    shift_grad, gain_grad = dp_total(
        jnp.stack([per_width(member, upstream), per_width(member, upstream * centered)])
    )
    source_grad = to_rows(member, gain_table * inverse) * (
        upstream
        - to_rows(member, shift_grad / totals)
        - centered * to_rows(member, gain_grad / totals)
    )
    return (source_grad, gain_grad, shift_grad)


def spatial_conv(source, kernel, stride):
    return lax.conv_general_dilated(
        source,
        kernel,
        (stride, stride),
        ((1, 1), (1, 1)),
        dimension_numbers=LAYOUT,
        preferred_element_type=jnp.float32,
    )


def spatial_input_grad(gradient, kernel, stride, side_cells):
    flipped = jnp.flip(kernel, (0, 1)).transpose(0, 1, 3, 2)
    upper_pad = 1 + (side_cells - 1) % stride
    return lax.conv_general_dilated(
        gradient,
        flipped,
        (1, 1),
        ((1, upper_pad), (1, upper_pad)),
        lhs_dilation=(stride, stride),
        dimension_numbers=LAYOUT,
        preferred_element_type=jnp.float32,
    )


def spatial_weight_grad(source, gradient, stride):
    outside = gradient.shape[1]
    padded = jnp.pad(source, ((0, 0), (1, 1), (1, 1), (0, 0)))
    grid_list = []
    for vertical in range(3):
        row_list = []
        for across in range(3):
            window = padded[
                :,
                vertical : vertical + stride * (outside - 1) + 1 : stride,
                across : across + stride * (outside - 1) + 1 : stride,
                :,
            ]
            row_list.append(
                jnp.einsum("bhwc,bhwd->cd", window, gradient, preferred_element_type=jnp.float32)
            )
        grid_list.append(jnp.stack(row_list))
    return jnp.stack(grid_list)


def spread_even(values):
    crops, height, breadth, channels = values.shape
    padded = jnp.pad(
        values[:, :, None, :, None, :], ((0, 0), (0, 0), (0, 1), (0, 0), (0, 1), (0, 0))
    )
    return padded.reshape(crops, 2 * height, 2 * breadth, channels)


def hidden_map(source, gain, shift, member, counts, channel_mask):
    normed, stored = norm_forward(source, gain, shift, member, counts)
    hidden = (jax.nn.silu(normed) * channel_mask).astype(jnp.bfloat16)
    return (hidden, normed, stored)


def pointwise(source, weight):
    return jnp.einsum("bhwc,cd->bhwd", source, weight, preferred_element_type=jnp.float32)


def pointwise_back(gradient, weight):
    return jnp.einsum("bhwd,cd->bhwc", gradient, weight, preferred_element_type=jnp.float32)


def pointwise_grad(source, gradient):
    return jnp.einsum(
        "bhwc,bhwd->cd", source, gradient, preferred_element_type=jnp.float32
    ).astype(jnp.bfloat16)


def expand_columns(weight, own):
    rows, columns = weight.shape
    blocks = relative(weight.reshape(rows, 4, columns // 4).transpose(1, 0, 2), own)
    return exchange_blocks(blocks).reshape(4 * rows, columns // 4)


def reduce_rows(weight, own):
    rows, columns = weight.shape
    blocks = exchange_blocks(relative(weight.reshape(4, rows // 4, columns), own))
    return blocks.transpose(1, 0, 2).reshape(rows // 4, 4 * columns)


def relative_rows(weight, own):
    rows, columns = weight.shape
    return relative(weight.reshape(4, rows // 4, columns), own).reshape(rows, columns)


def relative_taps(kernel, own):
    tall, wide, rows, columns = kernel.shape
    blocks = kernel.reshape(tall * wide, 4, rows // 4, columns).transpose(1, 0, 2, 3)
    return relative(blocks, own).transpose(1, 0, 2, 3).reshape(kernel.shape)


def shards(
    images,
    out_grad,
    crop_width,
    width_bound,
    depth_gate,
    first_reduce,
    first_reduce_gain,
    first_reduce_shift,
    first_spatial,
    first_spatial_gain,
    first_spatial_shift,
    first_expand,
    first_expand_gain,
    first_expand_shift,
    first_project,
    first_project_gain,
    first_project_shift,
    second_reduce,
    second_reduce_gain,
    second_reduce_shift,
    second_spatial,
    second_spatial_gain,
    second_spatial_shift,
    second_expand,
    second_expand_gain,
    second_expand_shift,
):
    own = lax.axis_index("chan")
    widths = width_bound.shape[0]
    member = (crop_width[:, None] == jnp.arange(widths, dtype=jnp.int32)[None, :]).astype(
        jnp.float32
    )
    middle = first_spatial.shape[3]
    offset = own * middle
    channel = (offset + jnp.arange(middle, dtype=jnp.int32)).astype(jnp.float32)
    bound_rows = jnp.dot(member, width_bound.astype(jnp.float32), precision=HIGHEST)
    width_mask = (channel[None, :] < bound_rows[:, None]).astype(jnp.float32)
    channel_mask = width_mask[:, None, None, :]
    gate_rows = jnp.dot(member, depth_gate.astype(jnp.float32), precision=HIGHEST)[
        :, None, None, None
    ]

    images_whole = gather_blocks(images)
    reduce_one = relative_rows(first_reduce, own)
    project = relative_rows(first_project, own)
    spatial_one = relative_taps(first_spatial, own)
    spatial_two = relative_taps(second_spatial, own)
    expand_one = expand_columns(first_expand, own)
    reduce_two = reduce_rows(second_reduce, own)
    expand_two = expand_columns(second_expand, own)

    counts = dp_total(jnp.broadcast_to(jnp.sum(member, axis=0)[:, None], (widths, middle)))[:, 0]
    reduced_one = pointwise(images_whole, reduce_one)
    hidden_a, normed_a, stored_a = hidden_map(
        reduced_one, first_reduce_gain, first_reduce_shift, member, counts, channel_mask
    )
    hidden_a_whole = gather_blocks(hidden_a)
    strided = images_whole[:, ::2, ::2, :]
    projected = pointwise(strided, project)
    spatial_out_one = spatial_conv(hidden_a_whole, spatial_one, 2)
    hidden_b, normed_b, stored_b = hidden_map(
        spatial_out_one, first_spatial_gain, first_spatial_shift, member, counts, channel_mask
    )
    hidden_b_whole = gather_blocks(hidden_b)
    expanded_one = pointwise(hidden_b_whole, expand_one)
    first_branch, stored_c = norm_forward(
        expanded_one, first_expand_gain, first_expand_shift, member, counts
    )
    shortcut, stored_p = norm_forward(
        projected, first_project_gain, first_project_shift, member, counts
    )
    first_pre = shortcut + first_branch
    first_out = jax.nn.silu(first_pre).astype(jnp.bfloat16)

    reduced_two = scatter_blocks(pointwise(first_out, reduce_two))
    hidden_d, normed_d, stored_d = hidden_map(
        reduced_two, second_reduce_gain, second_reduce_shift, member, counts, channel_mask
    )
    hidden_d_whole = gather_blocks(hidden_d)
    spatial_out_two = spatial_conv(hidden_d_whole, spatial_two, 1)
    hidden_e, normed_e, stored_e = hidden_map(
        spatial_out_two, second_spatial_gain, second_spatial_shift, member, counts, channel_mask
    )
    hidden_e_whole = gather_blocks(hidden_e)
    expanded_two = pointwise(hidden_e_whole, expand_two)
    second_branch, stored_f = norm_forward(
        expanded_two, second_expand_gain, second_expand_shift, member, counts
    )
    second_pre = first_out.astype(jnp.float32) + gate_rows * second_branch
    result = jax.nn.silu(second_pre).astype(jnp.bfloat16)

    second_delta = out_grad.astype(jnp.float32) * silu_slope(second_pre)
    expand_delta_two, gain_f, shift_f = norm_backward(
        second_delta * gate_rows, expanded_two, stored_f, second_expand_gain, member, counts
    )
    expand_delta_two = expand_delta_two.astype(jnp.bfloat16)
    hidden_e_grad = scatter_blocks(pointwise_back(expand_delta_two, expand_two))
    spatial_delta_two, gain_e, shift_e = norm_backward(
        hidden_e_grad * channel_mask * silu_slope(normed_e),
        spatial_out_two,
        stored_e,
        second_spatial_gain,
        member,
        counts,
    )
    spatial_delta_two = spatial_delta_two.astype(jnp.bfloat16)
    hidden_d_grad = scatter_blocks(
        spatial_input_grad(spatial_delta_two, spatial_two, 1, hidden_d.shape[1])
    )
    reduce_delta_two, gain_d, shift_d = norm_backward(
        hidden_d_grad * channel_mask * silu_slope(normed_d),
        reduced_two,
        stored_d,
        second_reduce_gain,
        member,
        counts,
    )
    reduce_delta_two = gather_blocks(reduce_delta_two.astype(jnp.bfloat16))
    carried = pointwise_back(reduce_delta_two, reduce_two)
    first_delta = (second_delta + carried) * silu_slope(first_pre)

    inputs, outputs = first_out.shape[3], expand_delta_two.shape[3]
    expand_two_grad = exchange_blocks(
        pointwise_grad(hidden_e_whole, expand_delta_two).reshape(4, middle, outputs)
    )
    reduce_two_grad = exchange_blocks(
        pointwise_grad(first_out, reduce_delta_two).reshape(inputs, 4, middle).transpose(1, 0, 2)
    )
    spatial_two_grad = (
        spatial_weight_grad(hidden_d_whole, spatial_delta_two, 1)
        .astype(jnp.bfloat16)
        .reshape(9, 4, middle, middle)
    )
    expand_two_grad, reduce_two_grad, spatial_two_grad = lax.psum(
        (expand_two_grad, reduce_two_grad, spatial_two_grad), "dp"
    )

    expand_delta_one, gain_c, shift_c = norm_backward(
        first_delta, expanded_one, stored_c, first_expand_gain, member, counts
    )
    project_delta, gain_p, shift_p = norm_backward(
        first_delta, projected, stored_p, first_project_gain, member, counts
    )
    expand_delta_one = expand_delta_one.astype(jnp.bfloat16)
    project_delta = project_delta.astype(jnp.bfloat16)
    hidden_b_grad = scatter_blocks(pointwise_back(expand_delta_one, expand_one))
    expand_one_grad = exchange_blocks(
        pointwise_grad(hidden_b_whole, expand_delta_one).reshape(4, middle, outputs)
    )
    project_grad = pointwise_grad(strided, project_delta)
    wide_grads = dp_sum_wide(
        jnp.concatenate([expand_one_grad.reshape(-1, outputs), project_grad], axis=0)
    )
    spatial_delta_one, gain_b, shift_b = norm_backward(
        hidden_b_grad * channel_mask * silu_slope(normed_b),
        spatial_out_one,
        stored_b,
        first_spatial_gain,
        member,
        counts,
    )
    spatial_delta_one = spatial_delta_one.astype(jnp.bfloat16)
    hidden_a_grad = scatter_blocks(
        spatial_input_grad(spatial_delta_one, spatial_one, 2, hidden_a.shape[1])
    )
    spatial_one_grad = dp_sum_wide(
        spatial_weight_grad(hidden_a_whole, spatial_delta_one, 2)
        .astype(jnp.bfloat16)
        .reshape(-1, middle)
    )
    reduce_delta_one, gain_a, shift_a = norm_backward(
        hidden_a_grad * channel_mask * silu_slope(normed_a),
        reduced_one,
        stored_a,
        first_reduce_gain,
        member,
        counts,
    )
    reduce_delta_one = reduce_delta_one.astype(jnp.bfloat16)
    reduce_one_grad = dp_sum_wide(pointwise_grad(images_whole, reduce_delta_one))
    projected_back = scatter_blocks(pointwise_back(project_delta, project))
    images_grad = scatter_blocks(pointwise_back(reduce_delta_one, reduce_one)) + spread_even(
        projected_back
    )

    def rows_back(grad, columns):
        blocks = grad.reshape(4, -1, columns)
        return relative(blocks, own).reshape(-1, columns).astype(jnp.float32)

    def columns_back(grad):
        blocks = relative(grad.reshape(4, middle, outputs), own)
        return blocks.transpose(1, 0, 2).reshape(middle, 4 * outputs).astype(jnp.float32)

    def taps_back(grad):
        blocks = grad.reshape(9, 4, middle, middle).transpose(1, 0, 2, 3)
        blocks = relative(blocks, own).transpose(1, 0, 2, 3)
        return blocks.reshape(3, 3, 4 * middle, middle).astype(jnp.float32)

    split = 4 * middle
    return (
        result,
        images_grad,
        rows_back(reduce_one_grad, middle),
        gain_a,
        shift_a,
        taps_back(spatial_one_grad),
        gain_b,
        shift_b,
        columns_back(wide_grads[:split]),
        gain_c,
        shift_c,
        rows_back(wide_grads[split:], outputs),
        gain_p,
        shift_p,
        rows_back(reduce_two_grad, middle),
        gain_d,
        shift_d,
        taps_back(spatial_two_grad),
        gain_e,
        shift_e,
        columns_back(expand_two_grad),
        gain_f,
        shift_f,
    )


def solution(mesh):
    placed = (
        P("dp", None, None, "chan"),
        P("dp", None, None, "chan"),
        P("dp"),
        P(),
        P(),
        P(None, "chan"),
        P(None, "chan"),
        P(None, "chan"),
        P(None, None, None, "chan"),
        P(None, "chan"),
        P(None, "chan"),
        P("chan", None),
        P(None, "chan"),
        P(None, "chan"),
        P(None, "chan"),
        P(None, "chan"),
        P(None, "chan"),
        P(None, "chan"),
        P(None, "chan"),
        P(None, "chan"),
        P(None, None, None, "chan"),
        P(None, "chan"),
        P(None, "chan"),
        P("chan", None),
        P(None, "chan"),
        P(None, "chan"),
    )
    return jax.shard_map(
        shards,
        mesh=mesh,
        in_specs=placed,
        out_specs=(
            P("dp", None, None, "chan"),
            P("dp", None, None, "chan"),
            P(None, "chan"),
            P(None, "chan"),
            P(None, "chan"),
            P(None, None, None, "chan"),
            P(None, "chan"),
            P(None, "chan"),
            P("chan", None),
            P(None, "chan"),
            P(None, "chan"),
            P(None, "chan"),
            P(None, "chan"),
            P(None, "chan"),
            P(None, "chan"),
            P(None, "chan"),
            P(None, "chan"),
            P(None, None, None, "chan"),
            P(None, "chan"),
            P(None, "chan"),
            P("chan", None),
            P(None, "chan"),
            P(None, "chan"),
        ),
        check_vma=False,
    )
```
